256 devices in a mesh: row: 16 (over x, z_lo), col: 16 (over z_hi, y, core).
Axes of the slice: x: 4, y: 4, z: 8 (z_hi: 2, z_lo: 4; z = z_hi * 4 + z_lo), core: 2. Of those that a mesh axis runs over, the one named last changes fastest.
Arguments:
- pair_block: bfloat16 [1024, 2048, 128], P('row', 'col'), may hold values from -6 to 6
- left_panel: bfloat16 [1024, 512, 128], P('row', 'col'), may hold values from -6 to 6
- right_panel: bfloat16 [2048, 512, 128], P('col', 'row'), may hold values from -6 to 6
- mask_left: int32 [1024, 512], P('row', 'col'), may hold values 0 or 1
- mask_right: int32 [2048, 512], P('col', 'row'), may hold values 0 or 1
- in_gain: float32 [128], replicated, may hold values from 0.1 to 1.9
- in_bias: float32 [128], replicated, may hold values from -3 to 3
- w_in: bfloat16 [128, 512], replicated, may hold values from -0.5 to 0.5
- out_gain: float32 [128], replicated, may hold values from 0.1 to 1.9
- out_bias: float32 [128], replicated, may hold values from -3 to 3
- w_gate_out: bfloat16 [128, 128], replicated, may hold values from -0.5 to 0.5
- w_out: bfloat16 [128, 128], replicated, may hold values from -0.5 to 0.5
Outputs:
- update: bfloat16 [1024, 2048, 128], P('row', 'col')
The draws below stay inside these ranges and needn't reach their ends.
All inputs are finite; a program needn't handle non-finite values. No bound on the sum of `mask_left` or of `mask_right` on one device may be relied on, other than what follows from the above.
Results may differ from the reference program's by a relative error of at most 0.0058.
Values may be sent and summed in bfloat16 or wider, within the bound.
No kernel may reach another device: no remote copies, remote signals or barrier semaphores. Data moves between devices by JAX's collectives and lax.ppermute only.
A program may use at most 128 MiB of HBM per device.

```python
import math
import jax
import jax.numpy as jnp
from jax import lax

C = 128
NI = 1024
NJ = 2048
NK = 512


def touch_ends(array, stream_key, smallest, top_value):
    shape = array.shape
    place = [jax.random.randint(jax.random.fold_in(stream_key, axis), (), 0, shape[axis]) for axis in range(len(shape))]
    array = array.at[tuple(place)].set(smallest)
    longest = shape.index(max(shape))
    place[longest] = (place[longest] + 1) % shape[longest]
    return array.at[tuple(place)].set(top_value)


def steps_of(rng, extent, split, low, high):
    def one(dim, parts):
        heights = jax.random.uniform(jax.random.fold_in(jax.random.fold_in(rng, 6), dim), (parts,), jnp.float32, low / len(split), high / len(split))
        return jnp.repeat(jnp.exp(heights), extent[dim] // parts).reshape((-1,) + (1,) * (len(extent) - dim - 1))

    level = one(*split[0])
    for cut in split[1:]:
        level = level * one(*cut)
    return level


def bell_draw(stream_key, extent, scale, reach, shards=(), held_as=jnp.bfloat16):
    loudness = steps_of(stream_key, extent, shards, -0.22, 0.18) if shards else 1.0
    values = jax.random.normal(stream_key, extent, jnp.float32) * scale * loudness
    return jnp.minimum(jnp.maximum(values, -reach), reach).astype(held_as)


def setup_inputs(seed: int = 0) -> dict:
    splits = jax.random.split(jax.random.key(seed), 13)
    return {
        "pair_block": bell_draw(splits[0], (NI, NJ, C), 1.0, 6.0, ((0, 16), (1, 16))),
        "left_panel": bell_draw(splits[1], (NI, NK, C), 1.0, 6.0, ((0, 16), (1, 16))),
        "right_panel": bell_draw(splits[2], (NJ, NK, C), 1.0, 6.0, ((0, 16), (1, 16))),
        "mask_left": touch_ends((jax.random.randint(splits[3], (NI, NK), 0, 8) < 7).astype(jnp.int32), jax.random.fold_in(splits[3], 1), 0, 1),
        "mask_right": touch_ends((jax.random.randint(splits[4], (NJ, NK), 0, 8) < 7).astype(jnp.int32), jax.random.fold_in(splits[4], 1), 0, 1),
        "in_gain": jnp.clip(1.0 + 0.18 * jax.random.normal(splits[5], (C,), jnp.float32), 0.1, 1.9),
        "in_bias": bell_draw(splits[6], (C,), 0.5, 3.0, (), jnp.float32),
        "w_in": bell_draw(splits[7], (C, 4 * C), C ** -0.5, 0.5),
        "out_gain": jnp.clip(1.0 + 0.18 * jax.random.normal(splits[8], (C,), jnp.float32), 0.1, 1.9),
        "out_bias": bell_draw(splits[9], (C,), 0.5, 3.0, (), jnp.float32),
        "w_gate_out": bell_draw(splits[10], (C, C), C ** -0.5, 0.5),
        "w_out": bell_draw(splits[11], (C, C), C ** -0.5, 0.5),
    }


def layer_norm(value, gain, bias):
    value = value.astype(jnp.float32)
    center = value - lax.optimization_barrier(jnp.mean(value, axis=-1, keepdims=True))
    spread = lax.optimization_barrier(jnp.mean(center * center, axis=-1, keepdims=True))
    return center * lax.rsqrt(spread + 1e-05) * gain + bias

def gated_side(panel, mask, in_gain, in_bias, weight):
    width = panel.shape[2]
    normed = layer_norm(panel, in_gain, in_bias).astype(jnp.bfloat16)
    flat = normed.reshape(-1, width)
    hidden = jnp.dot(flat, weight, preferred_element_type=jnp.float32)
    masked = mask.reshape(-1, 1).astype(jnp.float32)
    result = jax.nn.sigmoid(hidden[:, :width]) * hidden[:, width:] * masked
    return result.astype(jnp.bfloat16).reshape(panel.shape)

def reference(pair_block, left_panel, right_panel, mask_left, mask_right, in_gain, in_bias, w_in, out_gain, out_bias, w_gate_out, w_out):
    width = pair_block.shape[2]
    left_act = gated_side(left_panel, mask_left, in_gain, in_bias, w_in[:, 0:2 * width])
    right_act = gated_side(right_panel, mask_right, in_gain, in_bias, w_in[:, 2 * width:4 * width])
    right_wide = right_act.astype(jnp.float32)
    block = math.gcd(NI, 64)
    left_blocks = left_act.reshape(NI // block, block, NK, width)
    pair_blocks = pair_block.reshape(NI // block, block, NJ, width)

    def one_block(items):
        left_rows, pair_rows = items
        joined = jnp.einsum('ikc,jkc->ijc', left_rows.astype(jnp.float32), right_wide)
        joined_normed = layer_norm(joined, out_gain, out_bias).astype(jnp.bfloat16)
        normed_pair = layer_norm(pair_rows, in_gain, in_bias).astype(jnp.bfloat16)
        gate = jnp.dot(normed_pair.reshape(-1, width), w_gate_out, preferred_element_type=jnp.float32)
        value = jnp.dot(joined_normed.reshape(-1, width), w_out, preferred_element_type=jnp.float32)
        return (jax.nn.sigmoid(gate) * value).astype(jnp.bfloat16).reshape(block, NJ, width)
    output = lax.map(one_block, (left_blocks, pair_blocks))
    return output.reshape(NI, NJ, width)
```

```python
import jax
import jax.numpy as jnp
from jax import lax
from jax.experimental import pallas as pl
from jax.experimental.pallas import tpu as pltpu
from jax.sharding import Mesh, PartitionSpec as P

CHIPS = ("x", "zl", "zh", "y")
EPS = 1e-05
VMEM_LIMIT = 40 * 1024 * 1024


def layer_norm(value, gain, bias):
    center = value - jnp.mean(value, axis=-1, keepdims=True)
    spread = jnp.mean(center * center, axis=-1, keepdims=True)
    return center * lax.rsqrt(spread + EPS) * gain + bias


def prologue_kernel(
    left_ref, right_ref, mask_left_ref, mask_right_ref, gain_ref, bias_ref, w_ref, out_ref, act_ref, turned_ref
):
    gain = gain_ref[...]
    bias = bias_ref[...]

    def gated(block, weight):
        rows = block.shape[0] * block.shape[1]
        value = block.astype(jnp.float32).reshape(rows, 128)
        normed = layer_norm(value, gain, bias).astype(jnp.bfloat16)
        hidden = jnp.dot(normed, weight, preferred_element_type=jnp.float32)
        return jax.nn.sigmoid(hidden[:, :128]) * hidden[:, 128:]

    def right_block(b, carry):
        block = right_ref[pl.ds(b * 16, 16)]
        act_ref[pl.ds(pl.multiple_of(b * 512, 512), 512), :] = gated(block, w_ref[:, 256:512])
        return carry

    lax.fori_loop(0, 8, right_block, 0)

    def right_turn(k, carry):
        tile = act_ref[pl.ds(k, 128, stride=32), :]
        turned_ref[pl.ds(k, 128, stride=32), :] = tile.T * mask_right_ref[pl.ds(k, 1), :].astype(jnp.float32)
        return carry

    lax.fori_loop(0, 32, right_turn, 0)

    def right_out(b, carry):
        rows = turned_ref[pl.ds(pl.multiple_of(b * 256, 256), 256), :]
        out_ref[pl.ds(b * 8, 8), 0:32, :] = rows.reshape(8, 32, 128).astype(jnp.bfloat16)
        return carry

    lax.fori_loop(0, 16, right_out, 0)

    def left_block(b, carry):
        block = left_ref[pl.ds(b * 16, 16)]
        act_ref[pl.ds(pl.multiple_of(b * 512, 512), 512), :] = gated(block, w_ref[:, 0:256])
        return carry

    lax.fori_loop(0, 4, left_block, 0)

    def left_turn(k, carry):
        low = act_ref[pl.ds(k, 64, stride=32), :]
        high = act_ref[pl.ds(k + 16, 64, stride=32), :]
        tile = jnp.concatenate([low, high], axis=0)
        turned_ref[pl.ds(k, 128, stride=16), :] = tile.T * mask_left_ref[pl.ds(k, 1), :].astype(jnp.float32)
        return carry

    lax.fori_loop(0, 16, left_turn, 0)

    def left_out(b, carry):
        rows = turned_ref[pl.ds(pl.multiple_of(b * 256, 256), 256), :]
        out_ref[pl.ds(b * 16, 16), 32:48, :] = rows.reshape(16, 16, 128).astype(jnp.bfloat16)
        return carry

    lax.fori_loop(0, 8, left_out, 0)


def join_kernel(core_ref, own_ref, other_ref, out_ref, left_ref, right_ref):
    core = core_ref[0]
    lane = lax.broadcasted_iota(jnp.int32, (16, 128), 1)
    low_half = lane < 64

    def gather(t, carry):
        for side in range(2):
            block = 2 * t + (core if side == 0 else 1 - core)
            row = pl.multiple_of((side * 8 + t) * 32, 32)
            for jb in range(8):
                right_ref[pl.ds(row, 32), jb * 128 : (jb + 1) * 128] = own_ref[block * 8 + jb, 0:32, :]
            for pair in range(8):
                if side == 0:
                    even = own_ref[pair * 16 + t, 32:48, :]
                    odd = own_ref[pair * 16 + 8 + t, 32:48, :]
                else:
                    even = other_ref[pair * 16 + t]
                    odd = other_ref[pair * 16 + 8 + t]
                even = even.astype(jnp.float32)
                odd = odd.astype(jnp.float32)
                first = jnp.where(low_half, even, pltpu.roll(odd, 64, 1))
                second = jnp.where(low_half, pltpu.roll(even, 64, 1), odd)
                both = jnp.concatenate([first, second], axis=0).astype(jnp.bfloat16)
                left_ref[pl.ds(row, 32), pair * 128 : (pair + 1) * 128] = both
        return carry

    lax.fori_loop(0, 8, gather, 0)

    def multiply(b, carry):
        lhs = left_ref[:, pl.ds(pl.multiple_of(b * 256, 256), 256)]
        total = lax.dot_general(
            lhs, right_ref[...], (((0,), (0,)), ((), ())), preferred_element_type=jnp.float32
        )
        for q in range(4):
            for jb in range(8):
                out_ref[b * 4 + q, jb] = total[q * 64 : (q + 1) * 64, jb * 128 : (jb + 1) * 128].astype(jnp.bfloat16)
        return carry

    lax.fori_loop(0, 4, multiply, 0)


def gate_kernel(pair_ref, gain_ref, bias_ref, w_ref, out_ref):
    value = pair_ref[...].astype(jnp.float32).reshape(512, 128)
    normed = layer_norm(value, gain_ref[...], bias_ref[...]).astype(jnp.bfloat16)
    gate = jnp.dot(normed, w_ref[...], preferred_element_type=jnp.float32)
    out_ref[...] = jax.nn.sigmoid(gate)


def epilogue_kernel(joined_ref, gate_ref, gain_ref, bias_ref, w_ref, out_ref, wide_ref):
    joined = joined_ref[...].astype(jnp.float32)
    mean = jnp.mean(joined, axis=0)
    center = joined - mean[None]
    spread = jnp.mean(center * center, axis=0)
    normed = center * lax.rsqrt(spread + EPS)[None]
    wide_ref[...] = normed.reshape(128 * 16, 128)
    for i in range(16):
        tile = wide_ref[pl.ds(i, 128, stride=16), :]
        tile = (tile * gain_ref[...] + bias_ref[...]).astype(jnp.bfloat16)
        value = lax.dot_general(tile, w_ref[...], (((0,), (0,)), ((), ())), preferred_element_type=jnp.float32)
        out_ref[i] = (gate_ref[i * 128 : (i + 1) * 128, :] * value).astype(jnp.bfloat16)


def shards(
    pair_block,
    left_panel,
    right_panel,
    mask_left,
    mask_right,
    in_gain,
    in_bias,
    w_in,
    out_gain,
    out_bias,
    w_gate_out,
    w_out,
):
    params = pltpu.CompilerParams(vmem_limit_bytes=VMEM_LIMIT)
    gain_row = in_gain.reshape(1, 128)
    bias_row = in_bias.reshape(1, 128)
    mask_left_turned = mask_left.T.reshape(2, 16, 64).transpose(1, 0, 2).reshape(16, 128)
    packed = pl.pallas_call(
        prologue_kernel,
        out_shape=jax.ShapeDtypeStruct((128, 48, 128), jnp.bfloat16),
        scratch_shapes=[pltpu.VMEM((4096, 128), jnp.float32), pltpu.VMEM((4096, 128), jnp.float32)],
        compiler_params=params,
        cost_estimate=pl.CostEstimate(flops=2 * 6144 * 128 * 256, bytes_accessed=3 << 20, transcendentals=6144 * 128),
    )(left_panel, right_panel, mask_left_turned, mask_right.T, gain_row, bias_row, w_in)

    mine = lax.all_to_all(packed, CHIPS, split_axis=0, concat_axis=0, tiled=True)

    gate = pl.pallas_call(
        gate_kernel,
        grid=(16,),
        in_specs=[
            pl.BlockSpec((4, 128, 128), lambda b: (b, 0, 0)),
            pl.BlockSpec((1, 128), lambda b: (0, 0)),
            pl.BlockSpec((1, 128), lambda b: (0, 0)),
            pl.BlockSpec((128, 128), lambda b: (0, 0)),
        ],
        out_specs=pl.BlockSpec((512, 128), lambda b: (b, 0)),
        out_shape=jax.ShapeDtypeStruct((8192, 128), jnp.float32),
        compiler_params=params,
        cost_estimate=pl.CostEstimate(flops=2 * 8192 * 128 * 128, bytes_accessed=6 << 20, transcendentals=8192 * 128),
    )(pair_block, gain_row, bias_row, w_gate_out)

    other_left = lax.ppermute(mine[:, 32:48, :], "core", [(0, 1), (1, 0)])
    core = lax.axis_index("core").astype(jnp.int32).reshape(1)
    joined = pl.pallas_call(
        join_kernel,
        in_specs=[
            pl.BlockSpec(memory_space=pltpu.SMEM),
            pl.BlockSpec(memory_space=pltpu.VMEM),
            pl.BlockSpec(memory_space=pltpu.VMEM),
        ],
        out_shape=jax.ShapeDtypeStruct((16, 8, 64, 128), jnp.bfloat16),
        scratch_shapes=[pltpu.VMEM((512, 1024), jnp.bfloat16), pltpu.VMEM((512, 1024), jnp.bfloat16)],
        compiler_params=params,
        cost_estimate=pl.CostEstimate(flops=2 * 1024 * 1024 * 512, bytes_accessed=4 << 20, transcendentals=0),
    )(core, mine, other_left)

    home = lax.all_to_all(joined.reshape(128, 64, 128), CHIPS, split_axis=0, concat_axis=0, tiled=True)

    return pl.pallas_call(
        epilogue_kernel,
        grid=(4,),
        in_specs=[
            pl.BlockSpec((128, 16, 128), lambda b: (0, b, 0)),
            pl.BlockSpec((2048, 128), lambda b: (b, 0)),
            pl.BlockSpec((128, 1), lambda b: (0, 0)),
            pl.BlockSpec((128, 1), lambda b: (0, 0)),
            pl.BlockSpec((128, 128), lambda b: (0, 0)),
        ],
        out_specs=pl.BlockSpec((16, 128, 128), lambda b: (b, 0, 0)),
        out_shape=jax.ShapeDtypeStruct((64, 128, 128), jnp.bfloat16),
        scratch_shapes=[pltpu.VMEM((2048, 128), jnp.float32)],
        compiler_params=params,
        cost_estimate=pl.CostEstimate(flops=2 * 8192 * 128 * 128, bytes_accessed=8 << 20, transcendentals=0),
    )(home, gate, out_gain.reshape(128, 1), out_bias.reshape(128, 1), w_out)


def solution(mesh):
    fine = Mesh(mesh.devices.reshape(4, 4, 2, 4, 2), ("x", "zl", "zh", "y", "core"))
    row = ("x", "zl")
    col = ("zh", "y", "core")
    placed = (
        P(row, col, None),
        P(row, col, None),
        P(col, row, None),
        P(row, col),
        P(col, row),
        P(),
        P(),
        P(),
        P(),
        P(),
        P(),
        P(),
    )
    return jax.shard_map(shards, mesh=fine, in_specs=placed, out_specs=P(row, col, None), check_vma=False)
```

```python
import functools

import jax
import jax.numpy as jnp
from jax import lax
from jax.experimental import pallas as pl
from jax.experimental.pallas import tpu as pltpu
from jax.sharding import Mesh, PartitionSpec as P

CHIPS = ("x", "zl", "zh", "y")
EPS = 1e-05
VMEM_LIMIT = 40 * 1024 * 1024
PITCH = 40
HBM = pltpu.HBM


def layer_norm(value, gain, bias):
    center = value - jnp.mean(value, axis=-1, keepdims=True)
    spread = jnp.mean(center * center, axis=-1, keepdims=True)
    return center * lax.rsqrt(spread + EPS) * gain + bias


def prologue_kernel(
    left_hbm,
    right_hbm,
    mask_left_hbm,
    mask_right_hbm,
    gain_hbm,
    bias_hbm,
    w_hbm,
    out_ref,
    left_ref,
    right_ref,
    mask_left_ref,
    mask_right_ref,
    gain_ref,
    bias_ref,
    w_ref,
    act_ref,
    turned_ref,
    mask_ref,
    sems,
):
    right_copies = [
        pltpu.make_async_copy(right_hbm.at[pl.ds(b * 64, 64)], right_ref.at[pl.ds(b * 64, 64)], sems.at[b])
        for b in range(2)
    ]
    small_copies = [
        pltpu.make_async_copy(gain_hbm, gain_ref, sems.at[2]),
        pltpu.make_async_copy(bias_hbm, bias_ref, sems.at[3]),
        pltpu.make_async_copy(w_hbm, w_ref, sems.at[4]),
        pltpu.make_async_copy(mask_right_hbm, mask_right_ref, sems.at[5]),
        pltpu.make_async_copy(mask_left_hbm, mask_left_ref, sems.at[6]),
    ]
    left_copy = pltpu.make_async_copy(left_hbm, left_ref, sems.at[7])
    right_copies[0].start()
    for copy in small_copies:
        copy.start()
    right_copies[1].start()
    left_copy.start()
    ones = jnp.full((128, 128), 1 / 128, jnp.bfloat16)

    def norm_block(source, b, carry):
        flat = source[pl.ds(b * 16, 16)].reshape(512, 128)
        mean = jnp.dot(flat, ones, preferred_element_type=jnp.float32)
        center = flat.astype(jnp.float32) - mean
        spread = jnp.mean(center * center, axis=-1, keepdims=True)
        normed = center * lax.rsqrt(spread + EPS) * gain_ref[...] + bias_ref[...]
        for token in range(16):
            row = pl.multiple_of((b * 16 + token) * PITCH, 8)
            act_ref[pl.ds(row, 32), :] = normed[token * 32 : (token + 1) * 32]
        return carry

    def gated(tile, weight, mask):
        hidden = lax.dot_general(
            weight, tile.astype(jnp.bfloat16), (((0,), (1,)), ((), ())), preferred_element_type=jnp.float32
        )
        return (jnp.tanh(hidden[:128] * 0.5) * 0.5 + 0.5) * hidden[128:] * mask

    for copy in small_copies[:4]:
        copy.wait()
    for half in range(2):
        right_copies[half].wait()
        lax.fori_loop(half * 4, half * 4 + 4, functools.partial(norm_block, right_ref), 0, unroll=4)
    right_weight = w_ref[:, 256:512]

    def right_turn(k, carry):
        tile = act_ref[pl.ds(k, 128, stride=PITCH), :]
        mask = mask_right_ref[pl.ds(k, 1), :].astype(jnp.float32)
        turned_ref[pl.ds(k, 128, stride=PITCH), :] = gated(tile, right_weight, mask)
        return carry

    lax.fori_loop(0, 32, right_turn, 0, unroll=16)

    def right_out(b, carry):
        for q in range(8):
            row = pl.multiple_of((b * 8 + q) * PITCH, 8)
            out_ref[b * 8 + q, 0:32, :] = turned_ref[pl.ds(row, 32), :].astype(jnp.bfloat16)
        return carry

    lax.fori_loop(0, 16, right_out, 0, unroll=4)

    small_copies[4].wait()
    mask_left = mask_left_ref[...].astype(jnp.float32)
    mask_ref[...] = jnp.concatenate([mask_left[0:16], mask_left[16:32]], axis=1)
    left_copy.wait()
    lax.fori_loop(0, 4, functools.partial(norm_block, left_ref), 0, unroll=4)
    left_weight = w_ref[:, 0:256]

    def left_turn(k, carry):
        low = act_ref[pl.ds(k, 64, stride=PITCH), :]
        high = act_ref[pl.ds(k + 16, 64, stride=PITCH), :]
        tile = jnp.concatenate([low, high], axis=0)
        turned_ref[pl.ds(k, 128, stride=24), :] = gated(tile, left_weight, mask_ref[pl.ds(k, 1), :])
        return carry

    lax.fori_loop(0, 16, left_turn, 0, unroll=16)

    def left_out(b, carry):
        for q in range(8):
            row = pl.multiple_of((b * 8 + q) * 24, 8)
            out_ref[b * 8 + q, 32:48, :] = turned_ref[pl.ds(row, 16), :].astype(jnp.bfloat16)
        return carry

    lax.fori_loop(0, 16, left_out, 0, unroll=4)


def join_kernel(core_ref, own_ref, other_ref, out_ref, left_ref, right_ref):
    core = core_ref[0]
    lane = lax.broadcasted_iota(jnp.int32, (16, 128), 1)
    low_half = lane < 64

    def gather(t, carry):
        for side in range(2):
            block = 2 * t + (core if side == 0 else 1 - core)
            row = pl.multiple_of((side * 8 + t) * 32, 32)
            for jb in range(8):
                right_ref[pl.ds(row, 32), jb * 128 : (jb + 1) * 128] = own_ref[block * 8 + jb, 0:32, :]
            for pair in range(8):
                if side == 0:
                    even = own_ref[pair * 16 + t, 32:48, :]
                    odd = own_ref[pair * 16 + 8 + t, 32:48, :]
                else:
                    even = other_ref[pair * 16 + t]
                    odd = other_ref[pair * 16 + 8 + t]
                even = even.astype(jnp.float32)
                odd = odd.astype(jnp.float32)
                first = jnp.where(low_half, even, pltpu.roll(odd, 64, 1))
                second = jnp.where(low_half, pltpu.roll(even, 64, 1), odd)
                both = jnp.concatenate([first, second], axis=0).astype(jnp.bfloat16)
                left_ref[pl.ds(row, 32), pair * 128 : (pair + 1) * 128] = both
        return carry

    @pl.when(pl.program_id(0) == 0)
    def _():
        lax.fori_loop(0, 8, gather, 0, unroll=2)

    column = pl.multiple_of(pl.program_id(0) * 256, 256)
    total = lax.dot_general(
        left_ref[:, pl.ds(column, 256)], right_ref[...], (((0,), (0,)), ((), ())), preferred_element_type=jnp.float32
    )
    for q in range(4):
        for jb in range(8):
            out_ref[q * 8 + jb] = total[q * 64 : (q + 1) * 64, jb * 128 : (jb + 1) * 128].astype(jnp.bfloat16)


def gate_kernel(pair_ref, gain_ref, bias_ref, w_ref, out_ref):
    value = pair_ref[...].astype(jnp.float32).reshape(512, 128)
    normed = layer_norm(value, gain_ref[...], bias_ref[...]).astype(jnp.bfloat16)
    gate = jnp.dot(normed, w_ref[...], preferred_element_type=jnp.float32)
    out_ref[...] = jax.nn.sigmoid(gate)


def epilogue_kernel(joined_ref, gate_ref, gain_ref, bias_ref, w_ref, out_ref, wide_ref):
    gain = jnp.broadcast_to(gain_ref[...], (128, 128))
    bias = jnp.broadcast_to(bias_ref[...], (128, 128))
    zero = jnp.zeros((16, 128), jnp.float32)

    def total_of(c, total):
        value = joined_ref[c].astype(jnp.float32)
        wide_ref[pl.ds(pl.multiple_of(c * 24, 8), 16), :] = value
        return total + value

    mean = lax.fori_loop(0, 128, total_of, zero, unroll=16) * (1 / 128)

    def squares_of(c, total):
        center = wide_ref[pl.ds(pl.multiple_of(c * 24, 8), 16), :] - mean
        return total + center * center

    scale = lax.rsqrt(lax.fori_loop(0, 128, squares_of, zero, unroll=16) * (1 / 128) + EPS)
    for i in range(16):
        tile = wide_ref[pl.ds(i, 128, stride=24), :]
        tile = ((tile - mean[i : i + 1]) * scale[i : i + 1] * gain + bias).astype(jnp.bfloat16)
        value = lax.dot_general(tile, w_ref[...], (((0,), (0,)), ((), ())), preferred_element_type=jnp.float32)
        out_ref[i] = (gate_ref[i * 128 : (i + 1) * 128, :] * value).astype(jnp.bfloat16)


def shards(
    pair_block,
    left_panel,
    right_panel,
    mask_left,
    mask_right,
    in_gain,
    in_bias,
    w_in,
    out_gain,
    out_bias,
    w_gate_out,
    w_out,
):
    params = pltpu.CompilerParams(vmem_limit_bytes=VMEM_LIMIT)
    gain_row = in_gain.reshape(1, 128)
    bias_row = in_bias.reshape(1, 128)
    hbm = pl.BlockSpec(memory_space=HBM)
    packed = pl.pallas_call(
        prologue_kernel,
        in_specs=[hbm] * 7,
        out_shape=jax.ShapeDtypeStruct((128, 48, 128), jnp.bfloat16),
        scratch_shapes=[
            pltpu.VMEM((64, 32, 128), jnp.bfloat16),
            pltpu.VMEM((128, 32, 128), jnp.bfloat16),
            pltpu.VMEM((32, 64), jnp.int32),
            pltpu.VMEM((32, 128), jnp.int32),
            pltpu.VMEM((1, 128), jnp.float32),
            pltpu.VMEM((1, 128), jnp.float32),
            pltpu.VMEM((128, 512), jnp.bfloat16),
            pltpu.VMEM((128 * PITCH, 128), jnp.float32),
            pltpu.VMEM((128 * PITCH, 128), jnp.float32),
            pltpu.VMEM((16, 128), jnp.float32),
            pltpu.SemaphoreType.DMA((8,)),
        ],
        compiler_params=params,
        cost_estimate=pl.CostEstimate(flops=2 * 6144 * 128 * 256, bytes_accessed=3 << 20, transcendentals=6144 * 128),
    )(*[pltpu.with_memory_space_constraint(item, HBM) for item in (left_panel, right_panel, mask_left.T, mask_right.T, gain_row, bias_row, w_in)])

    mine = lax.all_to_all(packed, CHIPS, split_axis=0, concat_axis=0, tiled=True)

    gate = pl.pallas_call(
        gate_kernel,
        grid=(16,),
        in_specs=[
            pl.BlockSpec((4, 128, 128), lambda b: (b, 0, 0)),
            pl.BlockSpec((1, 128), lambda b: (0, 0)),
            pl.BlockSpec((1, 128), lambda b: (0, 0)),
            pl.BlockSpec((128, 128), lambda b: (0, 0)),
        ],
        out_specs=pl.BlockSpec((512, 128), lambda b: (b, 0)),
        out_shape=HBM((8192, 128), jnp.float32),
        compiler_params=params,
        cost_estimate=pl.CostEstimate(flops=2 * 8192 * 128 * 128, bytes_accessed=6 << 20, transcendentals=8192 * 128),
    )(pair_block, gain_row, bias_row, w_gate_out)

    other_left = lax.ppermute(mine[:, 32:48, :], "core", [(0, 1), (1, 0)])
    core = lax.axis_index("core").astype(jnp.int32).reshape(1)
    joined = pl.pallas_call(
        join_kernel,
        grid=(4,),
        in_specs=[
            pl.BlockSpec(memory_space=pltpu.SMEM),
            pl.BlockSpec(memory_space=pltpu.VMEM),
            pl.BlockSpec(memory_space=pltpu.VMEM),
        ],
        out_specs=pl.BlockSpec((32, 64, 128), lambda b: (b, 0, 0)),
        out_shape=HBM((128, 64, 128), jnp.bfloat16),
        scratch_shapes=[pltpu.VMEM((512, 1024), jnp.bfloat16), pltpu.VMEM((512, 1024), jnp.bfloat16)],
        compiler_params=params,
        cost_estimate=pl.CostEstimate(flops=2 * 1024 * 1024 * 512, bytes_accessed=4 << 20, transcendentals=0),
    )(core, mine, other_left)

    home = lax.all_to_all(joined, CHIPS, split_axis=0, concat_axis=0, tiled=True)

    return pl.pallas_call(
        epilogue_kernel,
        grid=(4,),
        in_specs=[
            pl.BlockSpec((128, 16, 128), lambda b: (0, b, 0)),
            pl.BlockSpec((2048, 128), lambda b: (b, 0)),
            pl.BlockSpec((128, 1), lambda b: (0, 0)),
            pl.BlockSpec((128, 1), lambda b: (0, 0)),
            pl.BlockSpec((128, 128), lambda b: (0, 0)),
        ],
        out_specs=pl.BlockSpec((16, 128, 128), lambda b: (b, 0, 0)),
        out_shape=jax.ShapeDtypeStruct((64, 128, 128), jnp.bfloat16),
        scratch_shapes=[pltpu.VMEM((128 * 24, 128), jnp.float32)],
        compiler_params=params,
        cost_estimate=pl.CostEstimate(flops=2 * 8192 * 128 * 128, bytes_accessed=8 << 20, transcendentals=0),
    )(home, pltpu.with_memory_space_constraint(gate, HBM), out_gain.reshape(128, 1), out_bias.reshape(128, 1), w_out)


def solution(mesh):
    fine = Mesh(mesh.devices.reshape(4, 4, 2, 4, 2), ("x", "zl", "zh", "y", "core"))
    row = ("x", "zl")
    col = ("zh", "y", "core")
    placed = (
        P(row, col, None),
        P(row, col, None),
        P(col, row, None),
        P(row, col),
        P(col, row),
        P(),
        P(),
        P(),
        P(),
        P(),
        P(),
        P(),
    )
    return jax.shard_map(shards, mesh=fine, in_specs=placed, out_specs=P(row, col, None), check_vma=False)
```

```python
import functools

import jax
import jax.numpy as jnp
from jax import lax
from jax.experimental import pallas as pl
from jax.experimental.pallas import tpu as pltpu
from jax.sharding import Mesh, PartitionSpec as P

CHIPS = ("x", "zl", "zh", "y")
EPS = 1e-05
VMEM_LIMIT = 40 * 1024 * 1024
PITCH = 40
HBM = pltpu.HBM


def layer_norm(value, gain, bias):
    center = value - jnp.mean(value, axis=-1, keepdims=True)
    spread = jnp.mean(center * center, axis=-1, keepdims=True)
    return center * lax.rsqrt(spread + EPS) * gain + bias


def prologue_kernel(
    left_hbm,
    right_hbm,
    mask_left_hbm,
    mask_right_hbm,
    gain_hbm,
    bias_hbm,
    w_hbm,
    out_ref,
    left_ref,
    right_ref,
    mask_left_ref,
    mask_right_ref,
    gain_ref,
    bias_ref,
    w_ref,
    act_ref,
    turned_ref,
    mask_ref,
    sems,
):
    right_copies = [
        pltpu.make_async_copy(right_hbm.at[pl.ds(b * 64, 64)], right_ref.at[pl.ds(b * 64, 64)], sems.at[b])
        for b in range(2)
    ]
    small_copies = [
        pltpu.make_async_copy(gain_hbm, gain_ref, sems.at[2]),
        pltpu.make_async_copy(bias_hbm, bias_ref, sems.at[3]),
        pltpu.make_async_copy(w_hbm, w_ref, sems.at[4]),
        pltpu.make_async_copy(mask_right_hbm, mask_right_ref, sems.at[5]),
        pltpu.make_async_copy(mask_left_hbm, mask_left_ref, sems.at[6]),
    ]
    left_copy = pltpu.make_async_copy(left_hbm, left_ref, sems.at[7])
    right_copies[0].start()
    for copy in small_copies:
        copy.start()
    right_copies[1].start()
    left_copy.start()
    ones = jnp.full((128, 128), 1 / 128, jnp.bfloat16)

    def norm_block(source, b, carry):
        flat = source[pl.ds(b * 16, 16)].reshape(512, 128)
        mean = jnp.dot(flat, ones, preferred_element_type=jnp.float32)
        center = flat.astype(jnp.float32) - mean
        spread = jnp.mean(center * center, axis=-1, keepdims=True)
        normed = center * lax.rsqrt(spread + EPS) * gain_ref[...] + bias_ref[...]
        for token in range(16):
            row = pl.multiple_of((b * 16 + token) * PITCH, 8)
            act_ref[pl.ds(row, 32), :] = normed[token * 32 : (token + 1) * 32]
        return carry

    def gated(tile, weight, mask):
        hidden = lax.dot_general(
            weight, tile.astype(jnp.bfloat16), (((0,), (1,)), ((), ())), preferred_element_type=jnp.float32
        )
        return (jnp.tanh(hidden[:128] * 0.5) * 0.5 + 0.5) * hidden[128:] * mask

    for copy in small_copies[:4]:
        copy.wait()
    for half in range(2):
        right_copies[half].wait()
        lax.fori_loop(half * 4, half * 4 + 4, functools.partial(norm_block, right_ref), 0, unroll=4)
    right_weight = w_ref[:, 256:512]

    def right_turn(k, carry):
        tile = act_ref[pl.ds(k, 128, stride=PITCH), :]
        mask = mask_right_ref[pl.ds(k, 1), :].astype(jnp.float32)
        turned_ref[pl.ds(k, 128, stride=PITCH), :] = gated(tile, right_weight, mask)
        return carry

    lax.fori_loop(0, 32, right_turn, 0, unroll=16)

    def right_out(b, carry):
        for q in range(8):
            row = pl.multiple_of((b * 8 + q) * PITCH, 8)
            out_ref[b * 8 + q, 0:32, :] = turned_ref[pl.ds(row, 32), :].astype(jnp.bfloat16)
        return carry

    lax.fori_loop(0, 16, right_out, 0, unroll=4)

    small_copies[4].wait()
    mask_left = mask_left_ref[...].astype(jnp.float32)
    mask_ref[...] = jnp.concatenate([mask_left[0:16], mask_left[16:32]], axis=1)
    left_copy.wait()
    lax.fori_loop(0, 4, functools.partial(norm_block, left_ref), 0, unroll=4)
    left_weight = w_ref[:, 0:256]

    def left_turn(k, carry):
        low = act_ref[pl.ds(k, 64, stride=PITCH), :]
        high = act_ref[pl.ds(k + 16, 64, stride=PITCH), :]
        tile = jnp.concatenate([low, high], axis=0)
        turned_ref[pl.ds(k, 128, stride=24), :] = gated(tile, left_weight, mask_ref[pl.ds(k, 1), :])
        return carry

    lax.fori_loop(0, 16, left_turn, 0, unroll=16)

    def left_out(b, carry):
        for q in range(8):
            row = pl.multiple_of((b * 8 + q) * 24, 8)
            out_ref[b * 8 + q, 32:48, :] = turned_ref[pl.ds(row, 16), :].astype(jnp.bfloat16)
        return carry

    lax.fori_loop(0, 16, left_out, 0, unroll=4)


def join_kernel(core_ref, own_ref, other_ref, out_ref, left_ref, right_ref):
    core = core_ref[0]
    lane = lax.broadcasted_iota(jnp.int32, (16, 128), 1)
    low_half = lane < 64

    def gather(t, carry):
        for side in range(2):
            block = 2 * t + (core if side == 0 else 1 - core)
            row = pl.multiple_of((side * 8 + t) * 32, 32)
            for jb in range(8):
                right_ref[pl.ds(row, 32), jb * 128 : (jb + 1) * 128] = own_ref[block * 8 + jb, 0:32, :]
            for pair in range(8):
                if side == 0:
                    even = own_ref[pair * 16 + t, 32:48, :]
                    odd = own_ref[pair * 16 + 8 + t, 32:48, :]
                else:
                    even = other_ref[pair * 16 + t]
                    odd = other_ref[pair * 16 + 8 + t]
                even = even.astype(jnp.float32)
                odd = odd.astype(jnp.float32)
                first = jnp.where(low_half, even, pltpu.roll(odd, 64, 1))
                second = jnp.where(low_half, pltpu.roll(even, 64, 1), odd)
                both = jnp.concatenate([first, second], axis=0).astype(jnp.bfloat16)
                left_ref[pl.ds(row, 32), pair * 128 : (pair + 1) * 128] = both
        return carry

    @pl.when(pl.program_id(0) == 0)
    def _():
        lax.fori_loop(0, 8, gather, 0, unroll=2)

    column = pl.multiple_of(pl.program_id(0) * 512, 512)
    total = lax.dot_general(
        left_ref[:, pl.ds(column, 512)], right_ref[...], (((0,), (0,)), ((), ())), preferred_element_type=jnp.float32
    )
    for q in range(8):
        for jb in range(8):
            out_ref[q * 8 + jb] = total[q * 64 : (q + 1) * 64, jb * 128 : (jb + 1) * 128].astype(jnp.bfloat16)


def gate_kernel(pair_ref, gain_ref, bias_ref, w_ref, out_ref):
    value = pair_ref[...].astype(jnp.float32).reshape(512, 128)
    normed = layer_norm(value, gain_ref[...], bias_ref[...]).astype(jnp.bfloat16)
    gate = jnp.dot(normed, w_ref[...], preferred_element_type=jnp.float32)
    out_ref[...] = jax.nn.sigmoid(gate)


def epilogue_kernel(joined_ref, gate_hbm, gain_ref, bias_ref, w_ref, out_ref, wide_ref, gate_ref, sems):
    step = pl.program_id(0)

    def gate_copy(part):
        rows = pl.ds(pl.multiple_of(part * 2048, 2048), 2048)
        return pltpu.make_async_copy(gate_hbm.at[rows], gate_ref.at[rows], sems.at[part])

    @pl.when(step == 0)
    def _():
        for part in range(4):
            gate_copy(part).start()

    gain = jnp.broadcast_to(gain_ref[...], (128, 128))
    bias = jnp.broadcast_to(bias_ref[...], (128, 128))
    zero = jnp.zeros((16, 128), jnp.float32)
    base = joined_ref[0].astype(jnp.float32)

    def totals_of(c, totals):
        shifted = joined_ref[c].astype(jnp.float32) - base
        wide_ref[pl.ds(pl.multiple_of(c * 24, 8), 16), :] = shifted
        return totals[0] + shifted, totals[1] + shifted * shifted

    total, squares = lax.fori_loop(0, 128, totals_of, (zero, zero), unroll=16)
    mean = total * (1 / 128)
    scale = lax.rsqrt(jnp.maximum(squares * (1 / 128) - mean * mean, 0.0) + EPS)
    gate_copy(step).wait()
    for i in range(16):
        tile = wide_ref[pl.ds(i, 128, stride=24), :]
        tile = ((tile - mean[i : i + 1]) * scale[i : i + 1] * gain + bias).astype(jnp.bfloat16)
        value = lax.dot_general(tile, w_ref[...], (((0,), (0,)), ((), ())), preferred_element_type=jnp.float32)
        gate = gate_ref[pl.ds(pl.multiple_of(step * 2048 + i * 128, 128), 128), :]
        out_ref[i] = (gate * value).astype(jnp.bfloat16)


def shards(
    pair_block,
    left_panel,
    right_panel,
    mask_left,
    mask_right,
    in_gain,
    in_bias,
    w_in,
    out_gain,
    out_bias,
    w_gate_out,
    w_out,
):
    params = pltpu.CompilerParams(vmem_limit_bytes=VMEM_LIMIT)
    gain_row = in_gain.reshape(1, 128)
    bias_row = in_bias.reshape(1, 128)
    hbm = pl.BlockSpec(memory_space=HBM)
    packed = pl.pallas_call(
        prologue_kernel,
        in_specs=[hbm] * 7,
        out_shape=jax.ShapeDtypeStruct((128, 48, 128), jnp.bfloat16),
        scratch_shapes=[
            pltpu.VMEM((64, 32, 128), jnp.bfloat16),
            pltpu.VMEM((128, 32, 128), jnp.bfloat16),
            pltpu.VMEM((32, 64), jnp.int32),
            pltpu.VMEM((32, 128), jnp.int32),
            pltpu.VMEM((1, 128), jnp.float32),
            pltpu.VMEM((1, 128), jnp.float32),
            pltpu.VMEM((128, 512), jnp.bfloat16),
            pltpu.VMEM((128 * PITCH, 128), jnp.float32),
            pltpu.VMEM((128 * PITCH, 128), jnp.float32),
            pltpu.VMEM((16, 128), jnp.float32),
            pltpu.SemaphoreType.DMA((8,)),
        ],
        compiler_params=params,
        cost_estimate=pl.CostEstimate(flops=2 * 6144 * 128 * 256, bytes_accessed=3 << 20, transcendentals=6144 * 128),
    )(*[pltpu.with_memory_space_constraint(item, HBM) for item in (left_panel, right_panel, mask_left.T, mask_right.T, gain_row, bias_row, w_in)])

    mine = lax.all_to_all(packed, CHIPS, split_axis=0, concat_axis=0, tiled=True)

    gate = pl.pallas_call(
        gate_kernel,
        grid=(16,),
        in_specs=[
            pl.BlockSpec((4, 128, 128), lambda b: (b, 0, 0)),
            pl.BlockSpec((1, 128), lambda b: (0, 0)),
            pl.BlockSpec((1, 128), lambda b: (0, 0)),
            pl.BlockSpec((128, 128), lambda b: (0, 0)),
        ],
        out_specs=pl.BlockSpec((512, 128), lambda b: (b, 0)),
        out_shape=HBM((8192, 128), jnp.float32),
        compiler_params=params,
        cost_estimate=pl.CostEstimate(flops=2 * 8192 * 128 * 128, bytes_accessed=6 << 20, transcendentals=8192 * 128),
    )(pair_block, gain_row, bias_row, w_gate_out)

    other_left = lax.ppermute(mine[:, 32:48, :], "core", [(0, 1), (1, 0)])
    core = lax.axis_index("core").astype(jnp.int32).reshape(1)
    joined = pl.pallas_call(
        join_kernel,
        grid=(2,),
        in_specs=[
            pl.BlockSpec(memory_space=pltpu.SMEM),
            pl.BlockSpec(memory_space=pltpu.VMEM),
            pl.BlockSpec(memory_space=pltpu.VMEM),
        ],
        out_specs=pl.BlockSpec((64, 64, 128), lambda b: (b, 0, 0)),
        out_shape=HBM((128, 64, 128), jnp.bfloat16),
        scratch_shapes=[pltpu.VMEM((512, 1024), jnp.bfloat16), pltpu.VMEM((512, 1024), jnp.bfloat16)],
        compiler_params=params,
        cost_estimate=pl.CostEstimate(flops=2 * 1024 * 1024 * 512, bytes_accessed=4 << 20, transcendentals=0),
    )(core, mine, other_left)

    home = lax.all_to_all(joined, CHIPS, split_axis=0, concat_axis=0, tiled=True)

    return pl.pallas_call(
        epilogue_kernel,
        grid=(4,),
        in_specs=[
            pl.BlockSpec((128, 16, 128), lambda b: (0, b, 0)),
            hbm,
            pl.BlockSpec((128, 1), lambda b: (0, 0)),
            pl.BlockSpec((128, 1), lambda b: (0, 0)),
            pl.BlockSpec((128, 128), lambda b: (0, 0)),
        ],
        out_specs=pl.BlockSpec((16, 128, 128), lambda b: (b, 0, 0)),
        out_shape=jax.ShapeDtypeStruct((64, 128, 128), jnp.bfloat16),
        scratch_shapes=[
            pltpu.VMEM((128 * 24, 128), jnp.float32),
            pltpu.VMEM((8192, 128), jnp.float32),
            pltpu.SemaphoreType.DMA((4,)),
        ],
        compiler_params=params,
        cost_estimate=pl.CostEstimate(flops=2 * 8192 * 128 * 128, bytes_accessed=8 << 20, transcendentals=0),
    )(home, pltpu.with_memory_space_constraint(gate, HBM), out_gain.reshape(128, 1), out_bias.reshape(128, 1), w_out)


def solution(mesh):
    fine = Mesh(mesh.devices.reshape(4, 4, 2, 4, 2), ("x", "zl", "zh", "y", "core"))
    row = ("x", "zl")
    col = ("zh", "y", "core")
    placed = (
        P(row, col, None),
        P(row, col, None),
        P(col, row, None),
        P(row, col),
        P(col, row),
        P(),
        P(),
        P(),
        P(),
        P(),
        P(),
        P(),
    )
    return jax.shard_map(shards, mesh=fine, in_specs=placed, out_specs=P(row, col, None), check_vma=False)
```

```python
import functools

import jax
import jax.numpy as jnp
from jax import lax
from jax.experimental import pallas as pl
from jax.experimental.pallas import tpu as pltpu
from jax.sharding import Mesh, PartitionSpec as P

CHIPS = ("x", "zl", "zh", "y")
EPS = 1e-05
VMEM_LIMIT = 40 * 1024 * 1024
PITCH = 40
HBM = pltpu.HBM


def layer_norm(value, gain, bias):
    center = value - jnp.mean(value, axis=-1, keepdims=True)
    spread = jnp.mean(center * center, axis=-1, keepdims=True)
    return center * lax.rsqrt(spread + EPS) * gain + bias


def prologue_kernel(
    left_hbm,
    right_hbm,
    mask_left_hbm,
    mask_right_hbm,
    gain_hbm,
    bias_hbm,
    w_hbm,
    out_hbm,
    right_out_ref,
    left_out_ref,
    left_ref,
    right_ref,
    mask_left_ref,
    mask_right_ref,
    gain_ref,
    bias_ref,
    w_ref,
    act_ref,
    turned_ref,
    mask_ref,
    sems,
):
    right_copies = [
        pltpu.make_async_copy(right_hbm.at[pl.ds(b * 64, 64)], right_ref.at[pl.ds(b * 64, 64)], sems.at[b])
        for b in range(2)
    ]
    small_copies = [
        pltpu.make_async_copy(gain_hbm, gain_ref, sems.at[2]),
        pltpu.make_async_copy(bias_hbm, bias_ref, sems.at[3]),
        pltpu.make_async_copy(w_hbm, w_ref, sems.at[4]),
        pltpu.make_async_copy(mask_right_hbm, mask_right_ref, sems.at[5]),
        pltpu.make_async_copy(mask_left_hbm, mask_left_ref, sems.at[6]),
    ]
    left_copy = pltpu.make_async_copy(left_hbm, left_ref, sems.at[7])
    out_copies = [
        pltpu.make_async_copy(
            source.at[pl.ds(half * 64, 64)],
            out_hbm.at[pl.ds(half * 64, 64), pl.ds(low, depth), :],
            sems.at[8 + part * 2 + half],
        )
        for part, (source, low, depth) in enumerate(((right_out_ref, 0, 32), (left_out_ref, 32, 16)))
        for half in range(2)
    ]
    right_copies[0].start()
    for copy in small_copies:
        copy.start()
    right_copies[1].start()
    left_copy.start()
    ones = jnp.full((128, 128), 1 / 128, jnp.bfloat16)

    def norm_block(source, b, carry):
        flat = source[pl.ds(b * 16, 16)].reshape(512, 128)
        mean = jnp.dot(flat, ones, preferred_element_type=jnp.float32)
        center = flat.astype(jnp.float32) - mean
        spread = jnp.mean(center * center, axis=-1, keepdims=True)
        normed = center * lax.rsqrt(spread + EPS) * gain_ref[...] + bias_ref[...]
        for token in range(16):
            row = pl.multiple_of((b * 16 + token) * PITCH, 8)
            act_ref[pl.ds(row, 32), :] = normed[token * 32 : (token + 1) * 32]
        return carry

    def gated(tile, weight, mask):
        hidden = lax.dot_general(
            weight, tile.astype(jnp.bfloat16), (((0,), (1,)), ((), ())), preferred_element_type=jnp.float32
        )
        return (jnp.tanh(hidden[:128] * 0.5) * 0.5 + 0.5) * hidden[128:] * mask

    for copy in small_copies[:4]:
        copy.wait()
    for half in range(2):
        right_copies[half].wait()
        lax.fori_loop(half * 4, half * 4 + 4, functools.partial(norm_block, right_ref), 0, unroll=4)
    right_weight = w_ref[:, 256:512]

    def right_turn(k, carry):
        tile = act_ref[pl.ds(k, 128, stride=PITCH), :]
        mask = mask_right_ref[pl.ds(k, 1), :].astype(jnp.float32)
        turned_ref[pl.ds(k, 128, stride=PITCH), :] = gated(tile, right_weight, mask)
        return carry

    lax.fori_loop(0, 32, right_turn, 0, unroll=16)

    def right_out(b, carry):
        for q in range(8):
            row = pl.multiple_of((b * 8 + q) * PITCH, 8)
            right_out_ref[b * 8 + q] = turned_ref[pl.ds(row, 32), :].astype(jnp.bfloat16)
        return carry

    for half in range(2):
        lax.fori_loop(half * 8, half * 8 + 8, right_out, 0, unroll=4)
        out_copies[half].start()

    small_copies[4].wait()
    mask_left = mask_left_ref[...].astype(jnp.float32)
    mask_ref[...] = jnp.concatenate([mask_left[0:16], mask_left[16:32]], axis=1)
    left_copy.wait()
    lax.fori_loop(0, 4, functools.partial(norm_block, left_ref), 0, unroll=4)
    left_weight = w_ref[:, 0:256]

    def left_turn(k, carry):
        low = act_ref[pl.ds(k, 64, stride=PITCH), :]
        high = act_ref[pl.ds(k + 16, 64, stride=PITCH), :]
        tile = jnp.concatenate([low, high], axis=0)
        turned_ref[pl.ds(k, 128, stride=24), :] = gated(tile, left_weight, mask_ref[pl.ds(k, 1), :])
        return carry

    lax.fori_loop(0, 16, left_turn, 0, unroll=16)

    def left_out(b, carry):
        for q in range(8):
            row = pl.multiple_of((b * 8 + q) * 24, 8)
            left_out_ref[b * 8 + q] = turned_ref[pl.ds(row, 16), :].astype(jnp.bfloat16)
        return carry

    for half in range(2):
        lax.fori_loop(half * 8, half * 8 + 8, left_out, 0, unroll=4)
        out_copies[2 + half].start()
    for copy in out_copies:
        copy.wait()


def join_kernel(core_ref, own_ref, other_ref, out_ref, left_ref, right_ref):
    core = core_ref[0]
    lane = lax.broadcasted_iota(jnp.int32, (16, 128), 1)
    low_half = lane < 64

    def gather(t, carry):
        for side in range(2):
            block = 2 * t + (core if side == 0 else 1 - core)
            row = pl.multiple_of((side * 8 + t) * 32, 32)
            for jb in range(8):
                right_ref[pl.ds(row, 32), jb * 128 : (jb + 1) * 128] = own_ref[block * 8 + jb, 0:32, :]
            for pair in range(8):
                if side == 0:
                    even = own_ref[pair * 16 + t, 32:48, :]
                    odd = own_ref[pair * 16 + 8 + t, 32:48, :]
                else:
                    even = other_ref[pair * 16 + t]
                    odd = other_ref[pair * 16 + 8 + t]
                even = even.astype(jnp.float32)
                odd = odd.astype(jnp.float32)
                first = jnp.where(low_half, even, pltpu.roll(odd, 64, 1))
                second = jnp.where(low_half, pltpu.roll(even, 64, 1), odd)
                both = jnp.concatenate([first, second], axis=0).astype(jnp.bfloat16)
                left_ref[pl.ds(row, 32), pair * 128 : (pair + 1) * 128] = both
        return carry

    @pl.when(pl.program_id(0) == 0)
    def _():
        lax.fori_loop(0, 8, gather, 0, unroll=2)

    column = pl.multiple_of(pl.program_id(0) * 512, 512)
    total = lax.dot_general(
        left_ref[:, pl.ds(column, 512)], right_ref[...], (((0,), (0,)), ((), ())), preferred_element_type=jnp.float32
    )
    for q in range(8):
        for jb in range(8):
            out_ref[q * 8 + jb] = total[q * 64 : (q + 1) * 64, jb * 128 : (jb + 1) * 128].astype(jnp.bfloat16)


def gate_kernel(pair_ref, gain_ref, bias_ref, w_ref, out_ref):
    value = pair_ref[...].astype(jnp.float32).reshape(512, 128)
    normed = layer_norm(value, gain_ref[...], bias_ref[...]).astype(jnp.bfloat16)
    gate = jnp.dot(normed, w_ref[...], preferred_element_type=jnp.float32)
    out_ref[...] = jax.nn.sigmoid(gate)


def epilogue_kernel(joined_ref, gate_hbm, gain_ref, bias_ref, w_ref, out_ref, wide_ref, gate_ref, sems):
    step = pl.program_id(0)

    def gate_copy(part):
        rows = pl.ds(pl.multiple_of(part * 2048, 2048), 2048)
        return pltpu.make_async_copy(gate_hbm.at[rows], gate_ref.at[rows], sems.at[part])

    @pl.when(step == 0)
    def _():
        for part in range(4):
            gate_copy(part).start()

    gain = jnp.broadcast_to(gain_ref[...], (128, 128)).T
    bias = jnp.broadcast_to(bias_ref[...], (128, 128)).T
    zero = jnp.zeros((16, 128), jnp.float32)
    base = joined_ref[0].astype(jnp.float32)

    def totals_of(c, totals):
        shifted = joined_ref[c].astype(jnp.float32) - base
        wide_ref[pl.ds(pl.multiple_of(c * 24, 8), 16), :] = shifted
        return totals[0] + shifted, totals[1] + shifted * shifted

    total, squares = lax.fori_loop(0, 128, totals_of, (zero, zero), unroll=16)
    mean = total * (1 / 128)
    scale = lax.rsqrt(jnp.maximum(squares * (1 / 128) - mean * mean, 0.0) + EPS)
    gate_copy(step).wait()
    for i in range(16):
        tile = wide_ref[pl.ds(i, 128, stride=24), :]
        tile = ((tile - mean[i : i + 1]) * scale[i : i + 1] * gain + bias).astype(jnp.bfloat16)
        value = lax.dot_general(tile, w_ref[...], (((0,), (0,)), ((), ())), preferred_element_type=jnp.float32)
        gate = gate_ref[pl.ds(pl.multiple_of(step * 2048 + i * 128, 128), 128), :]
        out_ref[i] = (gate * value).astype(jnp.bfloat16)


def shards(
    pair_block,
    left_panel,
    right_panel,
    mask_left,
    mask_right,
    in_gain,
    in_bias,
    w_in,
    out_gain,
    out_bias,
    w_gate_out,
    w_out,
):
    params = pltpu.CompilerParams(vmem_limit_bytes=VMEM_LIMIT)
    gain_row = in_gain.reshape(1, 128)
    bias_row = in_bias.reshape(1, 128)
    hbm = pl.BlockSpec(memory_space=HBM)
    packed = pl.pallas_call(
        prologue_kernel,
        in_specs=[hbm] * 7,
        out_specs=hbm,
        out_shape=HBM((128, 48, 128), jnp.bfloat16),
        scratch_shapes=[
            pltpu.VMEM((128, 32, 128), jnp.bfloat16),
            pltpu.VMEM((128, 16, 128), jnp.bfloat16),
            pltpu.VMEM((64, 32, 128), jnp.bfloat16),
            pltpu.VMEM((128, 32, 128), jnp.bfloat16),
            pltpu.VMEM((32, 64), jnp.int32),
            pltpu.VMEM((32, 128), jnp.int32),
            pltpu.VMEM((1, 128), jnp.float32),
            pltpu.VMEM((1, 128), jnp.float32),
            pltpu.VMEM((128, 512), jnp.bfloat16),
            pltpu.VMEM((129 * PITCH, 128), jnp.float32),
            pltpu.VMEM((129 * PITCH, 128), jnp.float32),
            pltpu.VMEM((16, 128), jnp.float32),
            pltpu.SemaphoreType.DMA((12,)),
        ],
        compiler_params=params,
        cost_estimate=pl.CostEstimate(flops=2 * 6144 * 128 * 256, bytes_accessed=3 << 20, transcendentals=6144 * 128),
    )(*[pltpu.with_memory_space_constraint(item, HBM) for item in (left_panel, right_panel, mask_left.T, mask_right.T, gain_row, bias_row, w_in)])

    mine = lax.all_to_all(packed, CHIPS, split_axis=0, concat_axis=0, tiled=True)

    gate = pl.pallas_call(
        gate_kernel,
        grid=(16,),
        in_specs=[
            pl.BlockSpec((4, 128, 128), lambda b: (b, 0, 0)),
            pl.BlockSpec((1, 128), lambda b: (0, 0)),
            pl.BlockSpec((1, 128), lambda b: (0, 0)),
            pl.BlockSpec((128, 128), lambda b: (0, 0)),
        ],
        out_specs=pl.BlockSpec((512, 128), lambda b: (b, 0)),
        out_shape=HBM((8192, 128), jnp.float32),
        compiler_params=params,
        cost_estimate=pl.CostEstimate(flops=2 * 8192 * 128 * 128, bytes_accessed=6 << 20, transcendentals=8192 * 128),
    )(pair_block, gain_row, bias_row, w_gate_out)

    mine, gate = lax.optimization_barrier((mine, gate))
    other_left = lax.ppermute(mine[:, 32:48, :], "core", [(0, 1), (1, 0)])
    core = lax.axis_index("core").astype(jnp.int32).reshape(1)
    joined = pl.pallas_call(
        join_kernel,
        grid=(2,),
        in_specs=[
            pl.BlockSpec(memory_space=pltpu.SMEM),
            pl.BlockSpec(memory_space=pltpu.VMEM),
            pl.BlockSpec(memory_space=pltpu.VMEM),
        ],
        out_specs=pl.BlockSpec((64, 64, 128), lambda b: (b, 0, 0)),
        out_shape=jax.ShapeDtypeStruct((128, 64, 128), jnp.bfloat16),
        scratch_shapes=[pltpu.VMEM((512, 1024), jnp.bfloat16), pltpu.VMEM((512, 1024), jnp.bfloat16)],
        compiler_params=params,
        cost_estimate=pl.CostEstimate(flops=2 * 1024 * 1024 * 512, bytes_accessed=4 << 20, transcendentals=0),
    )(core, mine, other_left)

    home = lax.all_to_all(joined, CHIPS, split_axis=0, concat_axis=0, tiled=True)

    return pl.pallas_call(
        epilogue_kernel,
        grid=(4,),
        in_specs=[
            pl.BlockSpec((128, 16, 128), lambda b: (0, b, 0)),
            hbm,
            pl.BlockSpec((1, 128), lambda b: (0, 0)),
            pl.BlockSpec((1, 128), lambda b: (0, 0)),
            pl.BlockSpec((128, 128), lambda b: (0, 0)),
        ],
        out_specs=pl.BlockSpec((16, 128, 128), lambda b: (b, 0, 0)),
        out_shape=jax.ShapeDtypeStruct((64, 128, 128), jnp.bfloat16),
        scratch_shapes=[
            pltpu.VMEM((129 * 24, 128), jnp.float32),
            pltpu.VMEM((8192, 128), jnp.float32),
            pltpu.SemaphoreType.DMA((4,)),
        ],
        compiler_params=params,
        cost_estimate=pl.CostEstimate(flops=2 * 8192 * 128 * 128, bytes_accessed=8 << 20, transcendentals=0),
    )(home, pltpu.with_memory_space_constraint(gate, HBM), out_gain.reshape(1, 128), out_bias.reshape(1, 128), w_out)


def solution(mesh):
    fine = Mesh(mesh.devices.reshape(4, 4, 2, 4, 2), ("x", "zl", "zh", "y", "core"))
    row = ("x", "zl")
    col = ("zh", "y", "core")
    placed = (
        P(row, col, None),
        P(row, col, None),
        P(col, row, None),
        P(row, col),
        P(col, row),
        P(),
        P(),
        P(),
        P(),
        P(),
        P(),
        P(),
    )
    return jax.shard_map(shards, mesh=fine, in_specs=placed, out_specs=P(row, col, None), check_vma=False)
```

```python
import functools

import jax
import jax.numpy as jnp
from jax import lax
from jax.experimental import pallas as pl
from jax.experimental.pallas import tpu as pltpu
from jax.sharding import Mesh, PartitionSpec as P

CHIPS = ("x", "zl", "zh", "y")
EPS = 1e-05
VMEM_LIMIT = 40 * 1024 * 1024
PITCH = 40
HBM = pltpu.HBM


def layer_norm(value, gain, bias):
    center = value - jnp.mean(value, axis=-1, keepdims=True)
    spread = jnp.mean(center * center, axis=-1, keepdims=True)
    return center * lax.rsqrt(spread + EPS) * gain + bias


def prologue_kernel(
    left_hbm,
    right_hbm,
    mask_left_hbm,
    mask_right_hbm,
    gain_hbm,
    bias_hbm,
    w_hbm,
    out_hbm,
    right_out_ref,
    left_out_ref,
    left_ref,
    right_ref,
    mask_left_ref,
    mask_right_ref,
    gain_ref,
    bias_ref,
    w_ref,
    act_ref,
    turned_ref,
    mask_ref,
    sems,
):
    right_copies = [
        pltpu.make_async_copy(right_hbm.at[pl.ds(b * 64, 64)], right_ref.at[pl.ds(b * 64, 64)], sems.at[b])
        for b in range(2)
    ]
    small_copies = [
        pltpu.make_async_copy(gain_hbm, gain_ref, sems.at[2]),
        pltpu.make_async_copy(bias_hbm, bias_ref, sems.at[3]),
        pltpu.make_async_copy(w_hbm, w_ref, sems.at[4]),
        pltpu.make_async_copy(mask_right_hbm, mask_right_ref, sems.at[5]),
        pltpu.make_async_copy(mask_left_hbm, mask_left_ref, sems.at[6]),
    ]
    left_copy = pltpu.make_async_copy(left_hbm, left_ref, sems.at[7])
    out_copies = [
        pltpu.make_async_copy(
            source.at[pl.ds(half * 64, 64)],
            out_hbm.at[pl.ds(half * 64, 64), pl.ds(low, depth), :],
            sems.at[8 + part * 2 + half],
        )
        for part, (source, low, depth) in enumerate(((right_out_ref, 0, 32), (left_out_ref, 32, 16)))
        for half in range(2)
    ]
    right_copies[0].start()
    for copy in small_copies:
        copy.start()
    right_copies[1].start()
    left_copy.start()
    ones = jnp.full((128, 128), 1 / 128, jnp.bfloat16)

    def norm_block(source, b, carry):
        flat = source[pl.ds(b * 16, 16)].reshape(512, 128)
        mean = jnp.dot(flat, ones, preferred_element_type=jnp.float32)
        center = flat.astype(jnp.float32) - mean
        spread = jnp.mean(center * center, axis=-1, keepdims=True)
        normed = center * lax.rsqrt(spread + EPS) * gain_ref[...] + bias_ref[...]
        for token in range(16):
            row = pl.multiple_of((b * 16 + token) * PITCH, 8)
            act_ref[pl.ds(row, 32), :] = normed[token * 32 : (token + 1) * 32]
        return carry

    def gated(tile, weight, mask):
        hidden = lax.dot_general(
            weight, tile.astype(jnp.bfloat16), (((0,), (1,)), ((), ())), preferred_element_type=jnp.float32
        )
        return (jnp.tanh(hidden[:128] * 0.5) * 0.5 + 0.5) * hidden[128:] * mask

    for copy in small_copies[:4]:
        copy.wait()
    for half in range(2):
        right_copies[half].wait()
        lax.fori_loop(half * 4, half * 4 + 4, functools.partial(norm_block, right_ref), 0, unroll=4)
    right_weight = w_ref[:, 256:512]

    def right_turn(k, carry):
        tile = act_ref[pl.ds(k, 128, stride=PITCH), :]
        mask = mask_right_ref[pl.ds(k, 1), :].astype(jnp.float32)
        turned_ref[pl.ds(k, 128, stride=PITCH), :] = gated(tile, right_weight, mask)
        return carry

    lax.fori_loop(0, 32, right_turn, 0, unroll=16)

    def right_out(b, carry):
        for q in range(8):
            row = pl.multiple_of((b * 8 + q) * PITCH, 8)
            right_out_ref[b * 8 + q] = turned_ref[pl.ds(row, 32), :].astype(jnp.bfloat16)
        return carry

    for half in range(2):
        lax.fori_loop(half * 8, half * 8 + 8, right_out, 0, unroll=4)
        out_copies[half].start()

    small_copies[4].wait()
    mask_left = mask_left_ref[...].astype(jnp.float32)
    mask_ref[...] = jnp.concatenate([mask_left[0:16], mask_left[16:32]], axis=1)
    left_copy.wait()
    lax.fori_loop(0, 4, functools.partial(norm_block, left_ref), 0, unroll=4)
    left_weight = w_ref[:, 0:256]

    def left_turn(k, carry):
        low = act_ref[pl.ds(k, 64, stride=PITCH), :]
        high = act_ref[pl.ds(k + 16, 64, stride=PITCH), :]
        tile = jnp.concatenate([low, high], axis=0)
        turned_ref[pl.ds(k, 128, stride=24), :] = gated(tile, left_weight, mask_ref[pl.ds(k, 1), :])
        return carry

    lax.fori_loop(0, 16, left_turn, 0, unroll=16)

    def left_out(b, carry):
        for q in range(8):
            row = pl.multiple_of((b * 8 + q) * 24, 8)
            left_out_ref[b * 8 + q] = turned_ref[pl.ds(row, 16), :].astype(jnp.bfloat16)
        return carry

    for half in range(2):
        lax.fori_loop(half * 8, half * 8 + 8, left_out, 0, unroll=4)
        out_copies[2 + half].start()
    for copy in out_copies:
        copy.wait()


def unfold_left(even, odd):
    low_half = lax.broadcasted_iota(jnp.int32, (16, 128), 1) < 64
    even = even.astype(jnp.float32)
    odd = odd.astype(jnp.float32)
    first = jnp.where(low_half, even, pltpu.roll(odd, 64, 1))
    second = jnp.where(low_half, pltpu.roll(even, 64, 1), odd)
    return jnp.concatenate([first, second], axis=0).astype(jnp.bfloat16)


def layout_kernel(core_ref, own_ref, right_ref, left_ref):
    core = core_ref[0]

    def gather(t, carry):
        row = pl.multiple_of(t * 32, 32)
        for side in range(2):
            block = 2 * t + (core if side == 0 else 1 - core)
            for jb in range(8):
                right_ref[pl.ds(side * 256 + row, 32), jb * 128 : (jb + 1) * 128] = own_ref[block * 8 + jb, 0:32, :]
        for pair in range(8):
            left_ref[pl.ds(row, 32), pair * 128 : (pair + 1) * 128] = unfold_left(
                own_ref[pair * 16 + t, 32:48, :], own_ref[pair * 16 + 8 + t, 32:48, :]
            )
        return carry

    lax.fori_loop(0, 8, gather, 0, unroll=2)


def join_kernel(own_left_ref, right_ref, other_ref, out_ref, left_ref):
    @pl.when(pl.program_id(0) == 0)
    def _():
        def gather(t, carry):
            row = pl.multiple_of(t * 32, 32)
            for pair in range(8):
                left_ref[pl.ds(row, 32), pair * 128 : (pair + 1) * 128] = unfold_left(
                    other_ref[pair * 16 + t], other_ref[pair * 16 + 8 + t]
                )
            return carry

        lax.fori_loop(0, 8, gather, 0, unroll=2)

    column = pl.multiple_of(pl.program_id(0) * 512, 512)
    lhs = jnp.concatenate([own_left_ref[:, pl.ds(column, 512)], left_ref[:, pl.ds(column, 512)]], axis=0)
    total = lax.dot_general(lhs, right_ref[...], (((0,), (0,)), ((), ())), preferred_element_type=jnp.float32)
    for q in range(8):
        for jb in range(8):
            out_ref[q * 8 + jb] = total[q * 64 : (q + 1) * 64, jb * 128 : (jb + 1) * 128].astype(jnp.bfloat16)


def gate_kernel(pair_ref, gain_ref, bias_ref, w_ref, out_ref):
    value = pair_ref[...].astype(jnp.float32).reshape(512, 128)
    normed = layer_norm(value, gain_ref[...], bias_ref[...]).astype(jnp.bfloat16)
    gate = jnp.dot(normed, w_ref[...], preferred_element_type=jnp.float32)
    out_ref[...] = jax.nn.sigmoid(gate)


def epilogue_kernel(joined_ref, gate_hbm, gain_ref, bias_ref, w_ref, out_ref, wide_ref, gate_ref, sems):
    step = pl.program_id(0)

    def gate_copy(part):
        rows = pl.ds(pl.multiple_of(part * 2048, 2048), 2048)
        return pltpu.make_async_copy(gate_hbm.at[rows], gate_ref.at[rows], sems.at[part])

    @pl.when(step == 0)
    def _():
        for part in range(4):
            gate_copy(part).start()

    gain = jnp.broadcast_to(gain_ref[...], (128, 128)).T
    bias = jnp.broadcast_to(bias_ref[...], (128, 128)).T
    zero = jnp.zeros((16, 128), jnp.float32)
    base = joined_ref[0].astype(jnp.float32)

    def totals_of(c, totals):
        shifted = joined_ref[c].astype(jnp.float32) - base
        wide_ref[pl.ds(pl.multiple_of(c * 24, 8), 16), :] = shifted
        return totals[0] + shifted, totals[1] + shifted * shifted

    total, squares = lax.fori_loop(0, 128, totals_of, (zero, zero), unroll=16)
    mean = total * (1 / 128)
    scale = lax.rsqrt(jnp.maximum(squares * (1 / 128) - mean * mean, 0.0) + EPS)
    gate_copy(step).wait()
    for i in range(16):
        tile = wide_ref[pl.ds(i, 128, stride=24), :]
        tile = ((tile - mean[i : i + 1]) * scale[i : i + 1] * gain + bias).astype(jnp.bfloat16)
        value = lax.dot_general(tile, w_ref[...], (((0,), (0,)), ((), ())), preferred_element_type=jnp.float32)
        gate = gate_ref[pl.ds(pl.multiple_of(step * 2048 + i * 128, 128), 128), :]
        out_ref[i] = (gate * value).astype(jnp.bfloat16)


def shards(
    pair_block,
    left_panel,
    right_panel,
    mask_left,
    mask_right,
    in_gain,
    in_bias,
    w_in,
    out_gain,
    out_bias,
    w_gate_out,
    w_out,
):
    params = pltpu.CompilerParams(vmem_limit_bytes=VMEM_LIMIT)
    gain_row = in_gain.reshape(1, 128)
    bias_row = in_bias.reshape(1, 128)
    hbm = pl.BlockSpec(memory_space=HBM)
    packed = pl.pallas_call(
        prologue_kernel,
        in_specs=[hbm] * 7,
        out_specs=hbm,
        out_shape=HBM((128, 48, 128), jnp.bfloat16),
        scratch_shapes=[
            pltpu.VMEM((128, 32, 128), jnp.bfloat16),
            pltpu.VMEM((128, 16, 128), jnp.bfloat16),
            pltpu.VMEM((64, 32, 128), jnp.bfloat16),
            pltpu.VMEM((128, 32, 128), jnp.bfloat16),
            pltpu.VMEM((32, 64), jnp.int32),
            pltpu.VMEM((32, 128), jnp.int32),
            pltpu.VMEM((1, 128), jnp.float32),
            pltpu.VMEM((1, 128), jnp.float32),
            pltpu.VMEM((128, 512), jnp.bfloat16),
            pltpu.VMEM((129 * PITCH, 128), jnp.float32),
            pltpu.VMEM((129 * PITCH, 128), jnp.float32),
            pltpu.VMEM((16, 128), jnp.float32),
            pltpu.SemaphoreType.DMA((12,)),
        ],
        compiler_params=params,
        cost_estimate=pl.CostEstimate(flops=2 * 6144 * 128 * 256, bytes_accessed=3 << 20, transcendentals=6144 * 128),
    )(*[pltpu.with_memory_space_constraint(item, HBM) for item in (left_panel, right_panel, mask_left.T, mask_right.T, gain_row, bias_row, w_in)])

    mine = lax.all_to_all(packed, CHIPS, split_axis=0, concat_axis=0, tiled=True)

    gate = pl.pallas_call(
        gate_kernel,
        grid=(16,),
        in_specs=[
            pl.BlockSpec((4, 128, 128), lambda b: (b, 0, 0)),
            pl.BlockSpec((1, 128), lambda b: (0, 0)),
            pl.BlockSpec((1, 128), lambda b: (0, 0)),
            pl.BlockSpec((128, 128), lambda b: (0, 0)),
        ],
        out_specs=pl.BlockSpec((512, 128), lambda b: (b, 0)),
        out_shape=HBM((8192, 128), jnp.float32),
        compiler_params=params,
        cost_estimate=pl.CostEstimate(flops=2 * 8192 * 128 * 128, bytes_accessed=6 << 20, transcendentals=8192 * 128),
    )(pair_block, gain_row, bias_row, w_gate_out)

    mine, gate = lax.optimization_barrier((mine, gate))
    other_left = lax.ppermute(mine[:, 32:48, :], "core", [(0, 1), (1, 0)])
    core = lax.axis_index("core").astype(jnp.int32).reshape(1)
    vmem = pl.BlockSpec(memory_space=pltpu.VMEM)
    right_matrix, own_left = pl.pallas_call(
        layout_kernel,
        in_specs=[pl.BlockSpec(memory_space=pltpu.SMEM), vmem],
        out_specs=[vmem, vmem],
        out_shape=[jax.ShapeDtypeStruct((512, 1024), jnp.bfloat16), jax.ShapeDtypeStruct((256, 1024), jnp.bfloat16)],
        compiler_params=params,
        cost_estimate=pl.CostEstimate(flops=1 << 20, bytes_accessed=3 << 20, transcendentals=0),
    )(core, mine)
    joined = pl.pallas_call(
        join_kernel,
        grid=(2,),
        in_specs=[vmem, vmem, vmem],
        out_specs=pl.BlockSpec((64, 64, 128), lambda b: (b, 0, 0)),
        out_shape=jax.ShapeDtypeStruct((128, 64, 128), jnp.bfloat16),
        scratch_shapes=[pltpu.VMEM((256, 1024), jnp.bfloat16)],
        compiler_params=params,
        cost_estimate=pl.CostEstimate(flops=2 * 1024 * 1024 * 512, bytes_accessed=4 << 20, transcendentals=0),
    )(own_left, right_matrix, other_left)

    home = lax.all_to_all(joined, CHIPS, split_axis=0, concat_axis=0, tiled=True)

    return pl.pallas_call(
        epilogue_kernel,
        grid=(4,),
        in_specs=[
            pl.BlockSpec((128, 16, 128), lambda b: (0, b, 0)),
            hbm,
            pl.BlockSpec((1, 128), lambda b: (0, 0)),
            pl.BlockSpec((1, 128), lambda b: (0, 0)),
            pl.BlockSpec((128, 128), lambda b: (0, 0)),
        ],
        out_specs=pl.BlockSpec((16, 128, 128), lambda b: (b, 0, 0)),
        out_shape=jax.ShapeDtypeStruct((64, 128, 128), jnp.bfloat16),
        scratch_shapes=[
            pltpu.VMEM((129 * 24, 128), jnp.float32),
            pltpu.VMEM((8192, 128), jnp.float32),
            pltpu.SemaphoreType.DMA((4,)),
        ],
        compiler_params=params,
        cost_estimate=pl.CostEstimate(flops=2 * 8192 * 128 * 128, bytes_accessed=8 << 20, transcendentals=0),
    )(home, pltpu.with_memory_space_constraint(gate, HBM), out_gain.reshape(1, 128), out_bias.reshape(1, 128), w_out)


def solution(mesh):
    fine = Mesh(mesh.devices.reshape(4, 4, 2, 4, 2), ("x", "zl", "zh", "y", "core"))
    row = ("x", "zl")
    col = ("zh", "y", "core")
    placed = (
        P(row, col, None),
        P(row, col, None),
        P(col, row, None),
        P(row, col),
        P(col, row),
        P(),
        P(),
        P(),
        P(),
        P(),
        P(),
        P(),
    )
    return jax.shard_map(shards, mesh=fine, in_specs=placed, out_specs=P(row, col, None), check_vma=False)
```
